256 devices in a mesh: dp: 64 (over z, x, core), tensor: 4 (over y).
Axes of the slice: x: 4, y: 4, z: 8, core: 2. Of those that a mesh axis runs over, the one named last changes fastest.
Arguments:
- inputs: bfloat16 [65536, 6144], P('dp'), may hold values from -6 to 6
- pre_act: bfloat16 [65536, 1024], P('dp', 'tensor'), may hold values from -6 to 6
- grad_hidden: bfloat16 [65536, 1024], P('dp', 'tensor'), may hold values from -6 to 6
- master: float32 [6144, 1024], P('dp', 'tensor'), may hold values from -0.1875 to 0.1875
- moment_one: float32 [6144, 1024], P('dp', 'tensor'), may hold values from -6 to 6
- moment_two: float32 [6144, 1024], P('dp', 'tensor'), may hold values from 1 to 262144
Outputs:
- grad_input: bfloat16 [65536, 6144], P('dp', 'tensor')
- new_master: float32 [6144, 1024], P('dp', 'tensor')
- new_one: float32 [6144, 1024], P('dp', 'tensor')
- new_two: float32 [6144, 1024], P('dp', 'tensor')
- new_weights: bfloat16 [6144, 1024], P(None, 'tensor')
The draws below stay inside these ranges and needn't reach their ends.
All inputs are finite; a program needn't handle non-finite values.
Results may differ from the reference program's by a relative error of at most 0.013.
Values may be sent and summed in bfloat16 or wider, within the bound.
No kernel may reach another device: no remote copies, remote signals or barrier semaphores. Data moves between devices by JAX's collectives and lax.ppermute only.
A program may use at most 128 MiB of HBM per device.

```python
import math
import jax
import jax.numpy as jnp
from jax import lax

D = 6144
BUCKET_DEV = 256
TOK_DEV = 1024
QBLOCK = 256
ADAM_STEP = 10
FF_W = 1024
TOKENS = 65536
N_DP = 64
N_TENSOR = 4


def block_scale(own_key, extent, pieces, low, high):
    def one(position, shards_of):
        draws = jax.random.uniform(jax.random.fold_in(jax.random.fold_in(own_key, 6), position), (shards_of,), jnp.float32, low / len(pieces), high / len(pieces))
        return jnp.repeat(jnp.exp(draws), extent[position] // shards_of).reshape((-1,) + (1,) * (len(extent) - position - 1))

    level = one(*pieces[0])
    for cut in pieces[1:]:
        level = level * one(*cut)
    return level


def scatter_about(own_key, extent, width, reach, cuts=(), kind=jnp.bfloat16):
    factor_of = block_scale(own_key, extent, cuts, -0.22, 0.18) if cuts else 1.0
    entries = jax.random.normal(own_key, extent, jnp.float32) * width * factor_of
    return jnp.minimum(jnp.maximum(entries, -reach), reach).astype(kind)


def setup_inputs(seed: int = 0) -> dict:
    splits = jax.random.split(jax.random.key(seed), 7)
    return {
        "inputs": scatter_about(splits[0], (TOKENS, D), 1.0, 6.0, ((0, 64),)),
        "pre_act": scatter_about(splits[1], (TOKENS, FF_W), 1.0, 6.0, ((0, 64), (1, 4))),
        "grad_hidden": scatter_about(splits[2], (TOKENS, FF_W), 1.0, 6.0, ((0, 64), (1, 4))),
        "master": scatter_about(splits[3], (D, FF_W), FF_W ** -0.5, 0.1875, ((0, 64), (1, 4)), jnp.float32),
        "moment_one": scatter_about(splits[4], (D, FF_W), 1.0, 6.0, ((0, 64), (1, 4)), jnp.float32),
        "moment_two": jnp.clip(jnp.exp(math.log(262144.0) - 12.476649 * jax.random.uniform(splits[5], (D, FF_W), jnp.float32) ** block_scale(splits[5], (D, FF_W), ((0, 64), (1, 4)), -0.2, 0.2)), 1.0, 262144.0),
    }


def gelu_slope(value):
    cdf = 0.5 * (1.0 + jax.scipy.special.erf(value / math.sqrt(2.0)))
    pdf = jnp.exp(-0.5 * value * value) / math.sqrt(2.0 * math.pi)
    return cdf + value * pdf

def quant_round(term):
    rows, cols = term.shape
    blocks = term.reshape(rows, cols // QBLOCK, QBLOCK)
    scale = (lax.optimization_barrier(jnp.max(jnp.abs(blocks), axis=2)) + 1e-06) / 127.0
    codes = jnp.clip(blocks / scale[:, :, None], -127.0, 127.0).astype(jnp.bfloat16)
    return (codes.astype(jnp.float32) * scale[:, :, None]).reshape(rows, cols)

def reference(inputs, pre_act, grad_hidden, master, moment_one, moment_two):
    act_grad = (grad_hidden.astype(jnp.float32) * gelu_slope(pre_act.astype(jnp.float32))).astype(jnp.bfloat16)
    weights = master.astype(jnp.bfloat16)
    act_blocks = act_grad.reshape(N_DP, TOK_DEV, FF_W)
    in_blocks = inputs.reshape(N_DP, TOK_DEV, D)

    def input_block(act_rows):
        total = jnp.zeros((TOK_DEV, D), jnp.float32)
        for index in range(N_TENSOR):
            cols = act_rows[:, index * BUCKET_DEV:(index + 1) * BUCKET_DEV]
            wcols = weights[:, index * BUCKET_DEV:(index + 1) * BUCKET_DEV]
            part = jnp.dot(cols, wcols.T, preferred_element_type=jnp.float32)
            total = total + part.astype(jnp.bfloat16).astype(jnp.float32)
        return total.astype(jnp.bfloat16)
    grad_input = lax.map(input_block, act_blocks).reshape(TOKENS, D)

    def add_term(carry, pair):
        term = jnp.dot(pair[0].T, pair[1], preferred_element_type=jnp.float32)
        return (carry + quant_round(term), None)
    grad, unused = lax.scan(add_term, jnp.zeros((D, FF_W), jnp.float32), (in_blocks, act_blocks))
    new_one = 0.9 * moment_one + 0.1 * grad
    new_two = 0.999 * moment_two + 0.001 * grad * grad
    corr_one = 1.0 - 0.9 ** ADAM_STEP
    corr_two = 1.0 - 0.999 ** ADAM_STEP
    update = new_one / corr_one / (jnp.sqrt(new_two / corr_two) + 1e-08) + 0.01 * master
    new_master = master - 0.01 * update
    return (grad_input, new_master, new_one, new_two, new_master.astype(jnp.bfloat16))
```

```python
import math

import jax
import jax.numpy as jnp
from jax import lax
from jax.experimental import pallas as pl
from jax.experimental.pallas import tpu as pltpu
from jax.sharding import PartitionSpec as P

ADAM_STEP = 10
NZ, NX, NC, NT = 8, 4, 2, 4
NDP = NZ * NX * NC
TOK = 1024
HID = 256
D = 6144
OWN = D // NDP
ZROWS = D // NZ
HALF = NZ * OWN

BF16 = jnp.bfloat16
F32 = jnp.float32


def dp_index(z, x, c):
    return (z * NX + x) * NC + c


POINTS = [(z, x, c) for z in range(NZ) for x in range(NX) for c in range(NC)]
CORE_SWAP = [(dp_index(z, x, c), dp_index(z, x, 1 - c)) for z, x, c in POINTS]
Z_GROUPS = [[dp_index(z, x, c) for z in range(NZ)] for x in range(NX) for c in range(NC)]
X_GROUPS = [[dp_index(z, x, c) for x in range(NX)] for z in range(NZ) for c in range(NC)]
PLANE = NDP // NT


def x_shift(s):
    return [(dp_index(z, x, c), dp_index(z, (x + s) % NX, c)) for z, x, c in POINTS]


def weight_route():
    pairs = []
    for r in range(NDP):
        for t in range(NT):
            k, j = divmod(r, PLANE)
            c, z = divmod(j, NZ)
            pairs.append((r * NT + t, dp_index(z, t, c) * NT + k))
    return pairs


def gelu_slope(value):
    cdf = 0.5 * (1.0 + jax.scipy.special.erf(value / math.sqrt(2.0)))
    pdf = jnp.exp(-0.5 * value * value) / math.sqrt(2.0 * math.pi)
    return cdf + value * pdf


def term_kernel(place, in_ref, act_ref, keep_ref, send_ref, held):
    x, c = place[0], place[1]
    term = lax.dot_general(
        in_ref[...], act_ref[...], (((0,), (0,)), ((), ())), preferred_element_type=F32
    )
    scale = (jnp.max(jnp.abs(term), axis=1, keepdims=True) + 1e-06) / 127.0
    codes = jnp.clip(term / scale, -127.0, 127.0).astype(BF16)
    held[...] = (codes.astype(F32) * scale).astype(BF16)
    for s in range(NX):
        base = lax.rem(x + s, NX) * (NC * OWN)
        mine = pl.multiple_of(base + c * OWN, OWN)
        other = pl.multiple_of(base + (1 - c) * OWN, OWN)
        keep_ref[s, 0] = held[pl.ds(mine, OWN), :]
        send_ref[s, 0] = held[pl.ds(other, OWN), :]


def make_terms(place, inputs, act_grad):
    out = jax.ShapeDtypeStruct((NX, NZ, OWN, HID), BF16)
    out_spec = pl.BlockSpec((NX, 1, OWN, HID), lambda i, place: (0, i, 0, 0))
    return pl.pallas_call(
        term_kernel,
        grid_spec=pltpu.PrefetchScalarGridSpec(
            num_scalar_prefetch=1,
            grid=(NZ,),
            in_specs=[
                pl.BlockSpec((TOK, ZROWS), lambda i, place: (0, i)),
                pl.BlockSpec((TOK, HID), lambda i, place: (0, 0)),
            ],
            out_specs=[out_spec, out_spec],
            scratch_shapes=[pltpu.VMEM((ZROWS, HID), BF16)],
        ),
        out_shape=[out, out],
        compiler_params=pltpu.CompilerParams(vmem_limit_bytes=40 * 2**20),
        cost_estimate=pl.CostEstimate(
            flops=2 * TOK * D * HID, bytes_accessed=2 * D * (TOK + HID), transcendentals=0
        ),
        name="terms",
    )(place, inputs, act_grad)


GI_ROWS = 256
GI_COLS = D // NT


def input_kernel(place, act_ref, mine_ref, other_ref, out_ref):
    c = place[1]
    for ref, core in ((mine_ref, c), (other_ref, 1 - c)):
        total = jnp.zeros((GI_ROWS, HALF), F32)
        for t in range(NT):
            total += lax.dot_general(
                act_ref[t], ref[t], (((1,), (1,)), ((), ())), preferred_element_type=F32
            )
        out_ref[:, pl.ds(pl.multiple_of(core * HALF, HALF), HALF)] = total.astype(BF16)


def make_grad_input(place, act_all, mine, other):
    whole = pl.BlockSpec((NT, HALF, HID), lambda i, place: (0, 0, 0))
    return pl.pallas_call(
        input_kernel,
        grid_spec=pltpu.PrefetchScalarGridSpec(
            num_scalar_prefetch=1,
            grid=(TOK // GI_ROWS,),
            in_specs=[
                pl.BlockSpec((NT, GI_ROWS, HID), lambda i, place: (0, i, 0)),
                whole,
                whole,
            ],
            out_specs=pl.BlockSpec((GI_ROWS, GI_COLS), lambda i, place: (i, 0)),
        ),
        out_shape=jax.ShapeDtypeStruct((TOK, GI_COLS), BF16),
        compiler_params=pltpu.CompilerParams(vmem_limit_bytes=40 * 2**20),
        cost_estimate=pl.CostEstimate(
            flops=2 * TOK * GI_COLS * HID * NT,
            bytes_accessed=2 * (TOK * HID * NT + GI_COLS * HID * NT + TOK * GI_COLS),
            transcendentals=0,
        ),
        name="grad_input",
    )(place, act_all, mine, other)


def place_kernel(place, *refs):
    pieces, out_ref, sems = refs[: 2 * NX], refs[2 * NX], refs[2 * NX + 1]
    x, c = place[0], place[1]
    copies = []
    for s in range(NX):
        from_x = lax.rem(x + NX - s, NX)
        for side, core in ((0, c), (1, 1 - c)):
            copy = pltpu.make_async_copy(
                pieces[2 * s + side], out_ref.at[:, from_x, core], sems.at[2 * s + side]
            )
            copy.start()
            copies.append(copy)
    for copy in copies:
        copy.wait()


def make_weights(place, pieces):
    anywhere = pl.BlockSpec(memory_space=pl.ANY)
    out = pl.pallas_call(
        place_kernel,
        in_specs=[pl.BlockSpec(memory_space=pltpu.SMEM)] + [anywhere] * (2 * NX),
        out_specs=anywhere,
        out_shape=jax.ShapeDtypeStruct((NZ, NX, NC, OWN, HID), BF16),
        scratch_shapes=[pltpu.SemaphoreType.DMA((2 * NX,))],
        name="place",
    )(place, *pieces)
    return out.reshape(D, HID)


def local(inputs, pre_act, grad_hidden, master, moment_one, moment_two):
    rank = lax.axis_index("dp")
    place = jnp.stack([lax.rem(lax.div(rank, NC), NX), lax.rem(rank, NC)]).astype(jnp.int32)

    act_grad = (grad_hidden.astype(F32) * gelu_slope(pre_act.astype(F32))).astype(BF16)
    act_all = lax.all_gather(act_grad, "tensor", axis=0)
    w_own = lax.ppermute(master.astype(BF16), ("dp", "tensor"), weight_route())

    keep, send = make_terms(place, inputs, act_grad)
    recv = lax.ppermute(send, "dp", CORE_SWAP)
    sums = [(keep[s].astype(F32) + recv[s].astype(F32)).astype(BF16) for s in range(NX)]
    parts = [lax.ppermute(sums[s], "dp", x_shift(s)) for s in range(1, NX)]

    w_own, _ = lax.optimization_barrier((w_own, sums[NX - 1]))
    w_z = lax.all_to_all(
        jnp.broadcast_to(w_own[None], (NZ, OWN, HID)),
        "dp",
        split_axis=0,
        concat_axis=0,
        axis_index_groups=Z_GROUPS,
        tiled=True,
    )
    w_mine = lax.all_gather(w_z.reshape(HALF, HID), "dp", axis=0, axis_index_groups=X_GROUPS)

    total = sums[0].astype(F32)
    for part in parts:
        total += part.astype(F32)
    blocks = lax.all_to_all(
        total.astype(BF16),
        "dp",
        split_axis=0,
        concat_axis=0,
        axis_index_groups=Z_GROUPS,
        tiled=True,
    )
    grad = jnp.sum(blocks.astype(F32), axis=0)

    new_one = 0.9 * moment_one + 0.1 * grad
    new_two = 0.999 * moment_two + 0.001 * grad * grad
    corr_one = 1.0 - 0.9**ADAM_STEP
    corr_two = 1.0 - 0.999**ADAM_STEP
    update = new_one / corr_one / (jnp.sqrt(new_two / corr_two) + 1e-08) + 0.01 * master
    new_master = master - 0.01 * update

    n_z = lax.all_to_all(
        jnp.broadcast_to(new_master.astype(BF16)[None], (NZ, OWN, HID)),
        "dp",
        split_axis=0,
        concat_axis=0,
        axis_index_groups=Z_GROUPS,
        tiled=True,
    )
    mine = [n_z] + [lax.ppermute(n_z, "dp", x_shift(s)) for s in range(1, NX)]
    other = [lax.ppermute(piece, "dp", CORE_SWAP) for piece in mine]
    new_weights = make_weights(place, [p for pair in zip(mine, other) for p in pair])

    w_other = lax.ppermute(w_mine, "dp", CORE_SWAP)
    grad_input = make_grad_input(place, act_all, w_mine, w_other)
    return (grad_input, new_master, new_one, new_two, new_weights)


def solution(mesh):
    shard = P("dp", "tensor")
    return jax.shard_map(
        local,
        mesh=mesh,
        in_specs=(P("dp", None), shard, shard, shard, shard, shard),
        out_specs=(shard, shard, shard, shard, P(None, "tensor")),
        check_vma=False,
    )
```

```python
import math

import jax
import jax.numpy as jnp
from jax import lax
from jax.experimental import pallas as pl
from jax.experimental.pallas import tpu as pltpu
from jax.sharding import PartitionSpec as P

ADAM_STEP = 10
NZ, NX, NC, NT = 8, 4, 2, 4
NDP = NZ * NX * NC
TOK = 1024
HID = 256
D = 6144
OWN = D // NDP
ZROWS = D // NZ
HALF = NZ * OWN

BF16 = jnp.bfloat16
F32 = jnp.float32


def dp_index(z, x, c):
    return (z * NX + x) * NC + c


POINTS = [(z, x, c) for z in range(NZ) for x in range(NX) for c in range(NC)]
CORE_SWAP = [(dp_index(z, x, c), dp_index(z, x, 1 - c)) for z, x, c in POINTS]
Z_GROUPS = [[dp_index(z, x, c) for z in range(NZ)] for x in range(NX) for c in range(NC)]
X_GROUPS = [[dp_index(z, x, c) for x in range(NX)] for z in range(NZ) for c in range(NC)]
PLANE = NDP // NT


def x_shift(s):
    return [(dp_index(z, x, c), dp_index(z, (x + s) % NX, c)) for z, x, c in POINTS]


def z_shift(s):
    return [(dp_index(z, x, c), dp_index((z + s) % NZ, x, c)) for z, x, c in POINTS]


def y_shift(s):
    return [(t, (t + s) % NT) for t in range(NT)]


def weight_route():
    pairs = []
    for r in range(NDP):
        for t in range(NT):
            k, j = divmod(r, PLANE)
            c, z = divmod(j, NZ)
            pairs.append((r * NT + t, dp_index(z, (t - k) % NX, c) * NT + k))
    return pairs


def gelu_slope(value):
    cdf = 0.5 * (1.0 + lax.erf(value * (1.0 / math.sqrt(2.0))))
    pdf = jnp.exp(-0.5 * value * value) * (1.0 / math.sqrt(2.0 * math.pi))
    return cdf + value * pdf


def term_kernel(
    place, pre_hbm, cot_hbm, in_ref, keep_ref, send_ref, act_ref, pre_ref, cot_ref, held, made, sems
):
    x, c = place[0], place[1]

    def fetch(i):
        columns = pl.ds(pl.multiple_of(i * ZROWS, ZROWS), ZROWS)
        return pltpu.make_async_copy(in_ref.at[:, columns], held.at[i], sems.at[i])

    pre_copy = pltpu.make_async_copy(pre_hbm, pre_ref, sems.at[NZ])
    cot_copy = pltpu.make_async_copy(cot_hbm, cot_ref, sems.at[NZ + 1])
    pre_copy.start()
    cot_copy.start()
    for i in range(NZ):
        fetch(i).start()
    pre_copy.wait()
    cot_copy.wait()
    slope = gelu_slope(pre_ref[...].astype(F32))
    act_ref[...] = (cot_ref[...].astype(F32) * slope).astype(BF16)

    @pl.loop(0, NZ)
    def _(i):
        fetch(i).wait()
        term = lax.dot_general(
            held[i], act_ref[...], (((0,), (0,)), ((), ())), preferred_element_type=F32
        )
        scale = (jnp.max(jnp.abs(term), axis=1, keepdims=True) + 1e-06) / 127.0
        codes = jnp.clip(term * (1.0 / scale), -127.0, 127.0).astype(BF16)
        made[...] = (codes.astype(F32) * scale).astype(BF16)
        for s in range(NX):
            base = lax.rem(x + s, NX) * (NC * OWN)
            mine = pl.multiple_of(base + c * OWN, OWN)
            other = pl.multiple_of(base + (1 - c) * OWN, OWN)
            keep_ref[s, i] = made[pl.ds(mine, OWN), :]
            send_ref[s, i] = made[pl.ds(other, OWN), :]


def make_terms(place, pre_act, grad_hidden, inputs):
    out = jax.ShapeDtypeStruct((NX, NZ, OWN, HID), BF16)
    vmem = pl.BlockSpec(memory_space=pltpu.VMEM)
    return pl.pallas_call(
        term_kernel,
        in_specs=[
            pl.BlockSpec(memory_space=pltpu.SMEM),
            pl.BlockSpec(memory_space=pltpu.HBM),
            pl.BlockSpec(memory_space=pltpu.HBM),
            pl.BlockSpec(memory_space=pltpu.HBM),
        ],
        out_specs=[vmem, vmem, vmem],
        out_shape=[out, out, jax.ShapeDtypeStruct((TOK, HID), BF16)],
        scratch_shapes=[
            pltpu.VMEM((TOK, HID), BF16),
            pltpu.VMEM((TOK, HID), BF16),
            pltpu.VMEM((NZ, TOK, ZROWS), BF16),
            pltpu.VMEM((ZROWS, HID), BF16),
            pltpu.SemaphoreType.DMA((NZ + 2,)),
        ],
        compiler_params=pltpu.CompilerParams(vmem_limit_bytes=40 * 2**20),
        cost_estimate=pl.CostEstimate(
            flops=2 * TOK * D * HID, bytes_accessed=2 * D * (TOK + HID), transcendentals=0
        ),
        name="terms",
    )(place, pre_act, grad_hidden, inputs)


GI_ROWS = 256
GI_COLS = D // NT


def input_kernel(place, *refs):
    x, c, z = place[0], place[1], place[2]
    act_refs, mine_refs, other_refs = refs[:NT], refs[NT : NT + NX], refs[NT + NX : NT + 2 * NX]
    out_ref, acts, weights = refs[NT + 2 * NX :]

    @pl.when(pl.program_id(0) == 0)
    def _():
        for s in range(NX):
            for i in range(NZ):
                j = lax.rem(z + NZ - i, NZ)
                weights[s, i * OWN : (i + 1) * OWN] = mine_refs[s][j]
                weights[NX + s, i * OWN : (i + 1) * OWN] = other_refs[s][j]

    for j in range(NT):
        acts[j] = act_refs[j][...]
    for side, core in ((0, c), (1, 1 - c)):
        total = jnp.zeros((GI_ROWS, HALF), F32)
        for s in range(NX):
            total += lax.dot_general(
                acts[lax.rem(s + NT - x, NT)],
                weights[side * NX + s],
                (((1,), (1,)), ((), ())),
                preferred_element_type=F32,
            )
        out_ref[:, pl.ds(pl.multiple_of(core * HALF, HALF), HALF)] = total.astype(BF16)


def make_grad_input(place, act_all, mine, other):
    whole = pl.BlockSpec((NZ, OWN, HID), lambda i, place: (0, 0, 0))
    return pl.pallas_call(
        input_kernel,
        grid_spec=pltpu.PrefetchScalarGridSpec(
            num_scalar_prefetch=1,
            grid=(TOK // GI_ROWS,),
            in_specs=[pl.BlockSpec((GI_ROWS, HID), lambda i, place: (i, 0))] * NT
            + [whole] * (2 * NX),
            out_specs=pl.BlockSpec((GI_ROWS, GI_COLS), lambda i, place: (i, 0)),
            scratch_shapes=[
                pltpu.VMEM((NT, GI_ROWS, HID), BF16),
                pltpu.VMEM((2 * NX, HALF, HID), BF16),
            ],
        ),
        out_shape=jax.ShapeDtypeStruct((TOK, GI_COLS), BF16),
        compiler_params=pltpu.CompilerParams(vmem_limit_bytes=40 * 2**20),
        cost_estimate=pl.CostEstimate(
            flops=2 * TOK * GI_COLS * HID * NT,
            bytes_accessed=2 * (TOK * HID * NT + GI_COLS * HID * NT + TOK * GI_COLS),
            transcendentals=0,
        ),
        name="grad_input",
    )(place, *act_all, *mine, *other)


def place_kernel(place, *refs):
    pieces, out_ref, sems = refs[: 2 * NX], refs[2 * NX], refs[2 * NX + 1]
    x, c = place[0], place[1]
    copies = []
    for s in range(NX):
        from_x = lax.rem(x + NX - s, NX)
        for side, core in ((0, c), (1, 1 - c)):
            copy = pltpu.make_async_copy(
                pieces[2 * s + side], out_ref.at[:, from_x, core], sems.at[2 * s + side]
            )
            copy.start()
            copies.append(copy)
    for copy in copies:
        copy.wait()


def make_weights(place, pieces):
    anywhere = pl.BlockSpec(memory_space=pl.ANY)
    out = pl.pallas_call(
        place_kernel,
        in_specs=[pl.BlockSpec(memory_space=pltpu.SMEM)]
        + [pl.BlockSpec(memory_space=pltpu.VMEM)] * (2 * NX),
        out_specs=anywhere,
        out_shape=jax.ShapeDtypeStruct((NZ, NX, NC, OWN, HID), BF16),
        scratch_shapes=[pltpu.SemaphoreType.DMA((2 * NX,))],
        compiler_params=pltpu.CompilerParams(vmem_limit_bytes=40 * 2**20),
        name="place",
    )(place, *pieces)
    return out.reshape(D, HID)


def swap_all_z(block):
    return lax.all_to_all(
        block, "dp", split_axis=0, concat_axis=0, axis_index_groups=Z_GROUPS, tiled=True
    )


def tie(*arrays):
    return lax.optimization_barrier(arrays)


def local(inputs, pre_act, grad_hidden, master, moment_one, moment_two):
    rank = lax.axis_index("dp")
    at_z, at_x = lax.div(rank, NX * NC), lax.rem(lax.div(rank, NC), NX)
    place = jnp.stack([at_x, lax.rem(rank, NC), at_z]).astype(jnp.int32)

    w_own = lax.ppermute(master.astype(BF16), ("dp", "tensor"), weight_route())
    keep, send, act_grad = make_terms(place, pre_act, grad_hidden, inputs)
    send, w_own = tie(send, w_own)

    recv = lax.ppermute(send, "dp", CORE_SWAP)
    sums = [(keep[s].astype(F32) + recv[s].astype(F32)).astype(BF16) for s in range(NX)]
    w_own, *sums = tie(w_own, *sums)
    parts = [lax.ppermute(sums[s], "dp", x_shift(s)) for s in range(1, NX)]
    w_z = [w_own] + [lax.ppermute(w_own, "dp", z_shift(s)) for s in range(1, NZ)]
    *parts, w_mine = tie(*parts, jnp.stack(w_z))
    total = sums[0].astype(F32)
    for part in parts:
        total += part.astype(F32)

    acts = [act_grad] + [lax.ppermute(act_grad, "tensor", y_shift(s)) for s in range(1, NT)]
    w_mine = [w_mine] + [lax.ppermute(w_mine, "dp", x_shift(s)) for s in range(1, NX)]
    blocks = swap_all_z(total.astype(BF16))
    blocks, acts[1], acts[3], w_mine[1], w_mine[3] = tie(
        blocks, acts[1], acts[3], w_mine[1], w_mine[3]
    )
    grad = jnp.sum(blocks.astype(F32), axis=0)

    new_one = 0.9 * moment_one + 0.1 * grad
    new_two = 0.999 * moment_two + 0.001 * grad * grad
    corr_one = 1.0 - 0.9**ADAM_STEP
    corr_two = 1.0 - 0.999**ADAM_STEP
    update = new_one / corr_one / (jnp.sqrt(new_two / corr_two) + 1e-08) + 0.01 * master
    new_master = master - 0.01 * update

    n_z = swap_all_z(jnp.broadcast_to(new_master.astype(BF16)[None], (NZ, OWN, HID)))
    n_z, acts[2], w_mine[2] = tie(n_z, acts[2], w_mine[2])
    w_other = [lax.ppermute(piece, "dp", CORE_SWAP) for piece in w_mine]
    mine = [n_z] + [lax.ppermute(n_z, "dp", x_shift(s)) for s in range(1, NX)]
    grad_input = make_grad_input(place, acts, w_mine, w_other)
    grad_input, *mine[1:] = tie(grad_input, *mine[1:])
    other = [lax.ppermute(piece, "dp", CORE_SWAP) for piece in mine]
    new_weights = make_weights(place, [p for pair in zip(mine, other) for p in pair])
    return (grad_input, new_master, new_one, new_two, new_weights)


def solution(mesh):
    shard = P("dp", "tensor")
    return jax.shard_map(
        local,
        mesh=mesh,
        in_specs=(P("dp", None), shard, shard, shard, shard, shard),
        out_specs=(shard, shard, shard, shard, P(None, "tensor")),
        check_vma=False,
    )
```

```python
import math

import jax
import jax.numpy as jnp
from jax import lax
from jax.experimental import pallas as pl
from jax.experimental.pallas import tpu as pltpu
from jax.sharding import PartitionSpec as P

ADAM_STEP = 10
NZ, NX, NC, NT = 8, 4, 2, 4
NDP = NZ * NX * NC
TOK = 1024
HID = 256
D = 6144
OWN = D // NDP
ZROWS = D // NZ
NJ = NZ // 2
HALF = NZ * OWN

BF16 = jnp.bfloat16
F32 = jnp.float32


def dp_index(z, x, c):
    return (z * NX + x) * NC + c


POINTS = [(z, x, c) for z in range(NZ) for x in range(NX) for c in range(NC)]
CORE_SWAP = [(dp_index(z, x, c), dp_index(z, x, 1 - c)) for z, x, c in POINTS]
PLANE = NDP // NT


def x_shift(s):
    return [(dp_index(z, x, c), dp_index(z, (x + s) % NX, c)) for z, x, c in POINTS]


def z_shift(s):
    return [(dp_index(z, x, c), dp_index((z + s) % NZ, x, c)) for z, x, c in POINTS]


Z_SWAP = [(dp_index(z, x, c), dp_index(z ^ 1, x, c)) for z, x, c in POINTS]


Z_GROUPS = [[dp_index(z, x, c) for z in range(NZ)] for x in range(NX) for c in range(NC)]


def weight_route():
    pairs = []
    for r in range(NDP):
        for t in range(NT):
            k, j = divmod(r, PLANE)
            c, z = divmod(j, NZ)
            pairs.append((r * NT + t, dp_index(z, t, c) * NT + k))
    return pairs


def gelu_slope(value):
    cdf = 0.5 * (1.0 + lax.erf(value * (1.0 / math.sqrt(2.0))))
    pdf = jnp.exp(-0.5 * value * value) * (1.0 / math.sqrt(2.0 * math.pi))
    return cdf + value * pdf


def position():
    rank = lax.axis_index("dp")
    return lax.rem(lax.div(rank, NC), NX), lax.rem(rank, NC), lax.div(rank, NX * NC)


def z_of(z, side, j):
    base = z if side == 0 else z + 1 - 2 * lax.rem(z, 2)
    return lax.rem(base + 2 * j, NZ)


def term_kernel(pre_hbm, cot_hbm, in_ref, *refs):
    keeps, sends, act_ref = refs[0:2], refs[2:4], refs[4]
    pre_ref, cot_ref, held, made, sems = refs[5:]
    x, c, z = position()

    def fetch(side, j):
        columns = pl.ds(pl.multiple_of(z_of(z, side, j) * ZROWS, ZROWS), ZROWS)
        slot = side * NJ + j
        return pltpu.make_async_copy(in_ref.at[:, columns], held.at[slot], sems.at[slot])

    pre_copy = pltpu.make_async_copy(pre_hbm, pre_ref, sems.at[NZ])
    cot_copy = pltpu.make_async_copy(cot_hbm, cot_ref, sems.at[NZ + 1])
    pre_copy.start()
    cot_copy.start()
    for side in (1, 0):
        for j in range(NJ):
            fetch(side, j).start()
    pre_copy.wait()
    cot_copy.wait()
    slope = gelu_slope(pre_ref[...].astype(F32))
    act_ref[...] = (cot_ref[...].astype(F32) * slope).astype(BF16)

    for side in (1, 0):

        @pl.loop(0, NJ)
        def _(j):
            fetch(side, j).wait()
            term = lax.dot_general(
                held[side * NJ + j],
                act_ref[...],
                (((0,), (0,)), ((), ())),
                preferred_element_type=F32,
            )
            scale = (jnp.max(jnp.abs(term), axis=1, keepdims=True) + 1e-06) / 127.0
            codes = jnp.clip(term * (1.0 / scale), -127.0, 127.0).astype(BF16)
            made[...] = (codes.astype(F32) * scale).astype(BF16)
            for s in range(NX):
                base = lax.rem(x + s, NX) * (NC * OWN)
                mine = pl.multiple_of(base + c * OWN, OWN)
                other = pl.multiple_of(base + (1 - c) * OWN, OWN)
                keeps[side][s, j] = made[pl.ds(mine, OWN), :]
                sends[side][s, j] = made[pl.ds(other, OWN), :]


def make_terms(pre_act, grad_hidden, inputs):
    out = jax.ShapeDtypeStruct((NX, NJ, OWN, HID), BF16)
    vmem = pl.BlockSpec(memory_space=pltpu.VMEM)
    hbm = pl.BlockSpec(memory_space=pltpu.HBM)
    return pl.pallas_call(
        term_kernel,
        in_specs=[hbm, hbm, hbm],
        out_specs=[vmem] * 5,
        out_shape=[out] * 4 + [jax.ShapeDtypeStruct((TOK, HID), BF16)],
        scratch_shapes=[
            pltpu.VMEM((TOK, HID), BF16),
            pltpu.VMEM((TOK, HID), BF16),
            pltpu.VMEM((NZ, TOK, ZROWS), BF16),
            pltpu.VMEM((ZROWS, HID), BF16),
            pltpu.SemaphoreType.DMA((NZ + 2,)),
        ],
        compiler_params=pltpu.CompilerParams(vmem_limit_bytes=56 * 2**20),
        cost_estimate=pl.CostEstimate(
            flops=2 * TOK * D * HID, bytes_accessed=2 * D * (TOK + HID), transcendentals=0
        ),
        name="terms",
    )(pre_act, grad_hidden, inputs)


GI_ROWS = 256
GI_COLS = D // NT


def input_kernel(act_ref, *refs):
    mine_refs, other_refs, out_ref = refs[:NX], refs[NX : 2 * NX], refs[2 * NX]
    x, c, _ = position()
    for w_refs, core in ((mine_refs, c), (other_refs, 1 - c)):
        total = jnp.zeros((GI_ROWS, HALF), F32)
        for s in range(NX):
            total += lax.dot_general(
                act_ref[lax.rem(x + NX - s, NX)],
                w_refs[s][...],
                (((1,), (1,)), ((), ())),
                preferred_element_type=F32,
            )
        out_ref[:, pl.ds(pl.multiple_of(core * HALF, HALF), HALF)] = total.astype(BF16)


def make_grad_input(act_all, mine, other):
    whole = pl.BlockSpec((HALF, HID), lambda i: (0, 0))
    return pl.pallas_call(
        input_kernel,
        grid=(TOK // GI_ROWS,),
        in_specs=[pl.BlockSpec((NT, GI_ROWS, HID), lambda i: (0, i, 0))] + [whole] * (2 * NX),
        out_specs=pl.BlockSpec((GI_ROWS, GI_COLS), lambda i: (i, 0)),
        out_shape=jax.ShapeDtypeStruct((TOK, GI_COLS), BF16),
        compiler_params=pltpu.CompilerParams(vmem_limit_bytes=40 * 2**20),
        cost_estimate=pl.CostEstimate(
            flops=2 * TOK * GI_COLS * HID * NT,
            bytes_accessed=2 * (TOK * HID * NT + GI_COLS * HID * NT + TOK * GI_COLS),
            transcendentals=0,
        ),
        name="grad_input",
    )(act_all, *mine, *other)


def collect_kernel(*refs):
    pieces, out_ref = refs[:NJ], refs[NJ]
    _, _, z = position()
    for j in range(NJ):
        for side in range(2):
            out_ref[z_of(z, side, NJ - j)] = pieces[j][side]


def collect(pieces):
    return pl.pallas_call(
        collect_kernel,
        out_shape=jax.ShapeDtypeStruct((NZ, OWN, HID), BF16),
        name="collect",
    )(*pieces)


def place_kernel(*refs):
    pieces, out_ref, sems = refs[: 2 * NX], refs[2 * NX], refs[2 * NX + 1]
    x, c, _ = position()
    copies = []
    for s in range(NX):
        from_x = lax.rem(x + NX - s, NX)
        for side, core in ((0, c), (1, 1 - c)):
            copy = pltpu.make_async_copy(
                pieces[2 * s + side], out_ref.at[:, from_x, core], sems.at[2 * s + side]
            )
            copy.start()
            copies.append(copy)
    for copy in copies:
        copy.wait()


def make_weights(pieces):
    out = pl.pallas_call(
        place_kernel,
        in_specs=[pl.BlockSpec(memory_space=pltpu.VMEM)] * (2 * NX),
        out_specs=pl.BlockSpec(memory_space=pl.ANY),
        out_shape=jax.ShapeDtypeStruct((NZ, NX, NC, OWN, HID), BF16),
        scratch_shapes=[pltpu.SemaphoreType.DMA((2 * NX,))],
        compiler_params=pltpu.CompilerParams(vmem_limit_bytes=40 * 2**20),
        name="place",
    )(*pieces)
    return out.reshape(D, HID)


def tie(*arrays):
    return lax.optimization_barrier(arrays)


def spread_kernel(in_ref, after_ref, out_ref):
    for i in range(out_ref.shape[0]):
        out_ref[i] = in_ref[...]


def spread(block, count, after):
    return pl.pallas_call(
        spread_kernel,
        in_specs=[pl.BlockSpec(memory_space=pltpu.VMEM), pl.BlockSpec(memory_space=pl.ANY)],
        out_shape=jax.ShapeDtypeStruct((count,) + block.shape, block.dtype),
        cost_estimate=pl.CostEstimate(flops=10**10, bytes_accessed=0, transcendentals=0),
        compiler_params=pltpu.CompilerParams(vmem_limit_bytes=40 * 2**20),
        name="spread",
    )(block, after)


def swap_all(blocks, axis, groups=None):
    return lax.all_to_all(
        blocks, axis, split_axis=0, concat_axis=0, axis_index_groups=groups, tiled=True
    )


def local(inputs, pre_act, grad_hidden, master, moment_one, moment_two):
    w_own = lax.ppermute(master, ("dp", "tensor"), weight_route())
    *made, act_grad = make_terms(pre_act, grad_hidden, inputs)
    keeps, sends = made[:2], made[2:]
    sends[0], sends[1], w_own = tie(sends[0], sends[1], w_own)
    w_spread = spread(w_own.astype(BF16), NZ, sends[1])

    sums = [None, None]
    for side in (1, 0):
        recv = lax.ppermute(sends[side], "dp", CORE_SWAP)
        sums[side] = [
            (keeps[side][s].astype(F32) + recv[s].astype(F32)).astype(BF16) for s in range(NX)
        ]
    w_z = swap_all(w_spread, "dp", Z_GROUPS).reshape(HALF, HID)
    totals = [None, None]
    for side in (1, 0):
        total = sums[side][0].astype(F32)
        for s in range(1, NX):
            total += lax.ppermute(sums[side][s], "dp", x_shift(s)).astype(F32)
        totals[side] = total
    ahead = totals[1].astype(BF16)
    other = lax.ppermute(ahead, "dp", Z_SWAP)
    act_all = swap_all(spread(act_grad, NT, w_z), "tensor").reshape(NT, TOK, HID)
    total = (totals[0] + other.astype(F32)).astype(BF16)
    total, w_z = tie(total, w_z)

    w_z = spread(w_z, 1, total)[0]
    w_mine = [w_z] + [lax.ppermute(w_z, "dp", x_shift(s)) for s in range(1, NX)]
    grad = total[0].astype(F32)
    for j in range(1, NJ):
        grad += lax.ppermute(total[j], "dp", z_shift(2 * j)).astype(F32)

    new_one = 0.9 * moment_one + 0.1 * grad
    new_two = 0.999 * moment_two + 0.001 * grad * grad
    corr_one = 1.0 - 0.9**ADAM_STEP
    corr_two = 1.0 - 0.999**ADAM_STEP
    update = new_one / corr_one / (jnp.sqrt(new_two / corr_two) + 1e-08) + 0.01 * master
    new_master = master - 0.01 * update

    n_own = new_master.astype(BF16)
    n_pair = jnp.stack([n_own, lax.ppermute(n_own, "dp", Z_SWAP)])
    n_z = [n_pair] + [lax.ppermute(n_pair, "dp", z_shift(2 * j)) for j in range(1, NJ)]
    n_z[2], act_all = tie(n_z[2], act_all)
    n_z, *w_mine = tie(collect(n_z), *w_mine)
    mine = [n_z] + [lax.ppermute(n_z, "dp", x_shift(s)) for s in range(1, NX)]
    w_other = [lax.ppermute(piece, "dp", CORE_SWAP) for piece in w_mine]
    grad_input = make_grad_input(act_all, w_mine, w_other)
    grad_input, *mine[1:] = tie(grad_input, *mine[1:])
    pieces = []
    for piece in mine:
        pieces += [piece, lax.ppermute(piece, "dp", CORE_SWAP)]
    new_weights = make_weights(pieces)
    return (grad_input, new_master, new_one, new_two, new_weights)


def solution(mesh):
    shard = P("dp", "tensor")
    return jax.shard_map(
        local,
        mesh=mesh,
        in_specs=(P("dp", None), shard, shard, shard, shard, shard),
        out_specs=(shard, shard, shard, shard, P(None, "tensor")),
        check_vma=False,
    )
```

```python
import math

import jax
import jax.numpy as jnp
from jax import lax
from jax.experimental import pallas as pl
from jax.experimental.pallas import tpu as pltpu
from jax.sharding import PartitionSpec as P

ADAM_STEP = 10
NZ, NX, NC, NT = 8, 4, 2, 4
NDP = NZ * NX * NC
TOK = 1024
HID = 256
D = 6144
OWN = D // NDP
ZROWS = D // NZ
NJ = NZ // 2
HALF = NZ * OWN

BF16 = jnp.bfloat16
F32 = jnp.float32


def dp_index(z, x, c):
    return (z * NX + x) * NC + c


POINTS = [(z, x, c) for z in range(NZ) for x in range(NX) for c in range(NC)]
CORE_SWAP = [(dp_index(z, x, c), dp_index(z, x, 1 - c)) for z, x, c in POINTS]
PLANE = NDP // NT


def x_shift(s):
    return [(dp_index(z, x, c), dp_index(z, (x + s) % NX, c)) for z, x, c in POINTS]


def z_shift(s):
    return [(dp_index(z, x, c), dp_index((z + s) % NZ, x, c)) for z, x, c in POINTS]


Z_SWAP = [(dp_index(z, x, c), dp_index(z ^ 1, x, c)) for z, x, c in POINTS]


Z_GROUPS = [[dp_index(z, x, c) for z in range(NZ)] for x in range(NX) for c in range(NC)]


def weight_route():
    pairs = []
    for r in range(NDP):
        for t in range(NT):
            k, j = divmod(r, PLANE)
            c, z = divmod(j, NZ)
            pairs.append((r * NT + t, dp_index(z, t, c) * NT + k))
    return pairs


def gelu_slope(value):
    cdf = 0.5 * (1.0 + lax.erf(value * (1.0 / math.sqrt(2.0))))
    pdf = jnp.exp(-0.5 * value * value) * (1.0 / math.sqrt(2.0 * math.pi))
    return cdf + value * pdf


def position():
    rank = lax.axis_index("dp")
    return lax.rem(lax.div(rank, NC), NX), lax.rem(rank, NC), lax.div(rank, NX * NC)


def z_of(z, side, j):
    base = z if side == 0 else z + 1 - 2 * lax.rem(z, 2)
    return lax.rem(base + 2 * j, NZ)


def term_kernel(pre_hbm, cot_hbm, in_ref, *refs):
    keeps, sends, act_ref, mark_ref = refs[0:2], refs[2:4], refs[4], refs[5]
    pre_ref, cot_ref, held, made, sems = refs[6:]
    mark_ref[...] = jnp.zeros_like(mark_ref)
    x, c, z = position()

    def fetch(side, j):
        columns = pl.ds(pl.multiple_of(z_of(z, side, j) * ZROWS, ZROWS), ZROWS)
        slot = side * NJ + j
        return pltpu.make_async_copy(in_ref.at[:, columns], held.at[slot], sems.at[slot])

    pre_copy = pltpu.make_async_copy(pre_hbm, pre_ref, sems.at[NZ])
    cot_copy = pltpu.make_async_copy(cot_hbm, cot_ref, sems.at[NZ + 1])
    pre_copy.start()
    cot_copy.start()
    for side in (1, 0):
        for j in range(NJ):
            fetch(side, j).start()
    pre_copy.wait()
    cot_copy.wait()
    slope = gelu_slope(pre_ref[...].astype(F32))
    act_ref[...] = (cot_ref[...].astype(F32) * slope).astype(BF16)

    for side in (1, 0):

        @pl.loop(0, NJ)
        def _(j):
            fetch(side, j).wait()
            term = lax.dot_general(
                held[side * NJ + j],
                act_ref[...],
                (((0,), (0,)), ((), ())),
                preferred_element_type=F32,
            )
            scale = (jnp.max(jnp.abs(term), axis=1, keepdims=True) + 1e-06) / 127.0
            codes = jnp.clip(term * (1.0 / scale), -127.0, 127.0).astype(BF16)
            made[...] = (codes.astype(F32) * scale).astype(BF16)
            for s in range(NX):
                base = lax.rem(x + s, NX) * (NC * OWN)
                mine = pl.multiple_of(base + c * OWN, OWN)
                other = pl.multiple_of(base + (1 - c) * OWN, OWN)
                keeps[side][s, j] = made[pl.ds(mine, OWN), :]
                sends[side][s, j] = made[pl.ds(other, OWN), :]


def make_terms(pre_act, grad_hidden, inputs):
    out = jax.ShapeDtypeStruct((NX, NJ, OWN, HID), BF16)
    vmem = pl.BlockSpec(memory_space=pltpu.VMEM)
    hbm = pl.BlockSpec(memory_space=pltpu.HBM)
    return pl.pallas_call(
        term_kernel,
        in_specs=[hbm, hbm, hbm],
        out_specs=[vmem] * 6,
        out_shape=[out] * 4
        + [jax.ShapeDtypeStruct((TOK, HID), BF16), jax.ShapeDtypeStruct((16, 128), BF16)],
        scratch_shapes=[
            pltpu.VMEM((TOK, HID), BF16),
            pltpu.VMEM((TOK, HID), BF16),
            pltpu.VMEM((NZ, TOK, ZROWS), BF16),
            pltpu.VMEM((ZROWS, HID), BF16),
            pltpu.SemaphoreType.DMA((NZ + 2,)),
        ],
        compiler_params=pltpu.CompilerParams(vmem_limit_bytes=56 * 2**20),
        cost_estimate=pl.CostEstimate(
            flops=2 * TOK * D * HID, bytes_accessed=2 * D * (TOK + HID), transcendentals=0
        ),
        name="terms",
    )(pre_act, grad_hidden, inputs)


GI_ROWS = 512
GI_COLS = D // NT


def input_kernel(act_ref, *refs):
    mine_refs, other_refs, out_ref = refs[:NX], refs[NX : 2 * NX], refs[2 * NX]
    x, c, _ = position()
    for w_refs, core in ((mine_refs, c), (other_refs, 1 - c)):
        total = jnp.zeros((GI_ROWS, HALF), F32)
        for s in range(NX):
            total += lax.dot_general(
                act_ref[lax.rem(x + NX - s, NX)],
                w_refs[s][...],
                (((1,), (1,)), ((), ())),
                preferred_element_type=F32,
            )
        out_ref[:, pl.ds(pl.multiple_of(core * HALF, HALF), HALF)] = total.astype(BF16)


def make_grad_input(act_all, mine, other):
    whole = pl.BlockSpec((HALF, HID), lambda i: (0, 0))
    return pl.pallas_call(
        input_kernel,
        grid=(TOK // GI_ROWS,),
        in_specs=[pl.BlockSpec((NT, GI_ROWS, HID), lambda i: (0, i, 0))] + [whole] * (2 * NX),
        out_specs=pl.BlockSpec((GI_ROWS, GI_COLS), lambda i: (i, 0)),
        out_shape=jax.ShapeDtypeStruct((TOK, GI_COLS), BF16),
        compiler_params=pltpu.CompilerParams(vmem_limit_bytes=40 * 2**20),
        cost_estimate=pl.CostEstimate(
            flops=TOK * GI_COLS, bytes_accessed=TOK * GI_COLS, transcendentals=0
        ),
        name="grad_input",
    )(act_all, *mine, *other)


def collect_kernel(*refs):
    pieces, out_ref = refs[:NJ], refs[NJ]
    _, _, z = position()
    for j in range(NJ):
        for side in range(2):
            out_ref[z_of(z, side, NJ - j)] = pieces[j][side]


def collect(pieces):
    return pl.pallas_call(
        collect_kernel,
        out_shape=jax.ShapeDtypeStruct((NZ, OWN, HID), BF16),
        compiler_params=pltpu.CompilerParams(vmem_limit_bytes=4 * 2**20),
        name="collect",
    )(*pieces)


def place_kernel(*refs):
    pieces, out_ref, sems = refs[: 2 * NX], refs[2 * NX], refs[2 * NX + 1]
    x, c, _ = position()
    copies = []
    for s in range(NX):
        from_x = lax.rem(x + NX - s, NX)
        for side, core in ((0, c), (1, 1 - c)):
            copy = pltpu.make_async_copy(
                pieces[2 * s + side], out_ref.at[:, from_x, core], sems.at[2 * s + side]
            )
            copy.start()
            copies.append(copy)
    for copy in copies:
        copy.wait()


def make_weights(pieces):
    out = pl.pallas_call(
        place_kernel,
        in_specs=[pl.BlockSpec(memory_space=pltpu.VMEM)] * (2 * NX),
        out_specs=pl.BlockSpec(memory_space=pl.ANY),
        out_shape=jax.ShapeDtypeStruct((NZ, NX, NC, OWN, HID), BF16),
        scratch_shapes=[pltpu.SemaphoreType.DMA((2 * NX,))],
        compiler_params=pltpu.CompilerParams(vmem_limit_bytes=40 * 2**20),
        name="place",
    )(*pieces)
    return out.reshape(D, HID)


def tie(*arrays):
    return lax.optimization_barrier(arrays)


def spread_kernel(in_ref, after_ref, out_ref):
    for i in range(out_ref.shape[0]):
        out_ref[i] = in_ref[...]


def spread(block, count, after):
    return pl.pallas_call(
        spread_kernel,
        in_specs=[pl.BlockSpec(memory_space=pltpu.VMEM), pl.BlockSpec(memory_space=pl.ANY)],
        out_shape=jax.ShapeDtypeStruct((count,) + block.shape, block.dtype),
        cost_estimate=pl.CostEstimate(flops=10**10, bytes_accessed=0, transcendentals=0),
        compiler_params=pltpu.CompilerParams(vmem_limit_bytes=40 * 2**20),
        name="spread",
    )(block, after)


def sum_kernel(*refs):
    *parts, out_ref = refs
    total = parts[0][...].astype(F32)
    for part in parts[1:]:
        total += part[...].astype(F32)
    out_ref[...] = total.astype(BF16)


def add_parts(*parts):
    return pl.pallas_call(
        sum_kernel,
        out_shape=jax.ShapeDtypeStruct(parts[0].shape, BF16),
        compiler_params=pltpu.CompilerParams(vmem_limit_bytes=8 * 2**20),
        name="add_parts",
    )(*parts)


def swap_all(blocks, axis, groups=None):
    return lax.all_to_all(
        blocks, axis, split_axis=0, concat_axis=0, axis_index_groups=groups, tiled=True
    )


def local(inputs, pre_act, grad_hidden, master, moment_one, moment_two):
    w_own = lax.ppermute(master, ("dp", "tensor"), weight_route())
    *made, act_grad, mark = make_terms(pre_act, grad_hidden, inputs)
    keeps, sends = made[:2], made[2:]
    sends[0], sends[1], w_own = tie(sends[0], sends[1], w_own)
    w_spread = spread(w_own.astype(BF16), NZ, mark)

    sums = [None, None]
    for side in (1, 0):
        recv = lax.ppermute(sends[side], "dp", CORE_SWAP)
        sums[side] = [
            (keeps[side][s].astype(F32) + recv[s].astype(F32)).astype(BF16) for s in range(NX)
        ]
    w_z = swap_all(w_spread, "dp", Z_GROUPS).reshape(HALF, HID)
    parts = [None, None]
    for side in (1, 0):
        parts[side] = [sums[side][0]] + [
            lax.ppermute(sums[side][s], "dp", x_shift(s)) for s in range(1, NX)
        ]
    ahead = add_parts(*parts[1])
    other = lax.ppermute(ahead, "dp", Z_SWAP)
    w_next = spread(w_z, 1, ahead)[0]
    act_all = swap_all(spread(act_grad, NT, w_next), "tensor").reshape(NT, TOK, HID)
    total = parts[0][0].astype(F32)
    for part in [*parts[0][1:], other]:
        total += part.astype(F32)
    total = total.astype(BF16)
    w_near = [lax.ppermute(w_next, "dp", x_shift(s)) for s in (1, NX - 1)]
    w_far = lax.ppermute(spread(w_z, 1, total)[0], "dp", x_shift(2))
    others = [lax.ppermute(total[j], "dp", z_shift(2 * j)) for j in range(1, NJ)]
    others[-1], *w_near = tie(others[-1], *w_near)
    grad = total[0].astype(F32)
    for part in others:
        grad += part.astype(F32)

    new_one = 0.9 * moment_one + 0.1 * grad
    new_two = 0.999 * moment_two + 0.001 * grad * grad
    corr_one = 1.0 - 0.9**ADAM_STEP
    corr_two = 1.0 - 0.999**ADAM_STEP
    update = new_one / corr_one / (jnp.sqrt(new_two / corr_two) + 1e-08) + 0.01 * master
    new_master = master - 0.01 * update

    n_own = new_master.astype(BF16)
    n_pair = jnp.stack([n_own, lax.ppermute(n_own, "dp", Z_SWAP)])
    n_z = [n_pair] + [lax.ppermute(n_pair, "dp", z_shift(2 * j)) for j in range(1, NJ)]
    n_z[2], act_all = tie(n_z[2], act_all)
    n_z, w_far = tie(collect(n_z), w_far)
    mine = [n_z] + [lax.ppermute(n_z, "dp", x_shift(s)) for s in range(1, NX)]
    mine[1], w_z, w_far, *w_near = tie(mine[1], w_z, w_far, *w_near)
    w_mine = [w_z, w_near[0], w_far, w_near[1]]
    w_other = [lax.ppermute(piece, "dp", CORE_SWAP) for piece in w_mine]
    grad_input = make_grad_input(act_all, w_mine, w_other)
    pieces = []
    for piece in mine:
        pieces += [piece, lax.ppermute(piece, "dp", CORE_SWAP)]
    grad_input, *pieces = tie(grad_input, *pieces)
    new_weights = make_weights(pieces)
    return (grad_input, new_master, new_one, new_two, new_weights)


def solution(mesh):
    shard = P("dp", "tensor")
    return jax.shard_map(
        local,
        mesh=mesh,
        in_specs=(P("dp", None), shard, shard, shard, shard, shard),
        out_specs=(shard, shard, shard, shard, P(None, "tensor")),
        check_vma=False,
    )
```

```python
import math

import jax
import jax.numpy as jnp
from jax import lax
from jax.experimental import pallas as pl
from jax.experimental.pallas import tpu as pltpu
from jax.sharding import PartitionSpec as P

ADAM_STEP = 10
NZ, NX, NC, NT = 8, 4, 2, 4
NDP = NZ * NX * NC
TOK = 1024
HID = 256
D = 6144
OWN = D // NDP
ZROWS = D // NZ
NJ = NZ // 2
HALF = NZ * OWN

BF16 = jnp.bfloat16
F32 = jnp.float32


def dp_index(z, x, c):
    return (z * NX + x) * NC + c


POINTS = [(z, x, c) for z in range(NZ) for x in range(NX) for c in range(NC)]
CORE_SWAP = [(dp_index(z, x, c), dp_index(z, x, 1 - c)) for z, x, c in POINTS]
PLANE = NDP // NT


def x_shift(s):
    return [(dp_index(z, x, c), dp_index(z, (x + s) % NX, c)) for z, x, c in POINTS]


def z_shift(s):
    return [(dp_index(z, x, c), dp_index((z + s) % NZ, x, c)) for z, x, c in POINTS]


Z_SWAP = [(dp_index(z, x, c), dp_index(z ^ 1, x, c)) for z, x, c in POINTS]


Z_GROUPS = [[dp_index(z, x, c) for z in range(NZ)] for x in range(NX) for c in range(NC)]


def weight_route():
    pairs = []
    for r in range(NDP):
        for t in range(NT):
            k, j = divmod(r, PLANE)
            c, z = divmod(j, NZ)
            pairs.append((r * NT + t, dp_index(z, t, c) * NT + k))
    return pairs


def gelu_slope(value):
    cdf = 0.5 * (1.0 + lax.erf(value * (1.0 / math.sqrt(2.0))))
    pdf = jnp.exp(-0.5 * value * value) * (1.0 / math.sqrt(2.0 * math.pi))
    return cdf + value * pdf


def position():
    rank = lax.axis_index("dp")
    return lax.rem(lax.div(rank, NC), NX), lax.rem(rank, NC), lax.div(rank, NX * NC)


def z_of(z, side, j):
    base = z if side == 0 else z + 1 - 2 * lax.rem(z, 2)
    return lax.rem(base + 2 * j, NZ)


def term_kernel(pre_hbm, cot_hbm, in_ref, *refs):
    keeps, sends, acts_hbm, mark_ref = refs[0:2], refs[2:4], refs[4], refs[5]
    act_ref, pre_ref, cot_ref, held, made, sems = refs[6:]
    mark_ref[...] = jnp.zeros_like(mark_ref)
    x, c, z = position()

    def fetch(side, j):
        columns = pl.ds(pl.multiple_of(z_of(z, side, j) * ZROWS, ZROWS), ZROWS)
        slot = side * NJ + j
        return pltpu.make_async_copy(in_ref.at[:, columns], held.at[slot], sems.at[slot])

    pre_copy = pltpu.make_async_copy(pre_hbm, pre_ref, sems.at[NZ])
    cot_copy = pltpu.make_async_copy(cot_hbm, cot_ref, sems.at[NZ + 1])
    pre_copy.start()
    cot_copy.start()
    for side in (1, 0):
        for j in range(NJ):
            fetch(side, j).start()
    pre_copy.wait()
    cot_copy.wait()
    slope = gelu_slope(pre_ref[...].astype(F32))
    act_ref[...] = (cot_ref[...].astype(F32) * slope).astype(BF16)
    act_copies = [
        pltpu.make_async_copy(act_ref, acts_hbm.at[t], sems.at[NZ + 2 + t]) for t in range(NT)
    ]
    for copy in act_copies:
        copy.start()

    for side in (1, 0):

        @pl.loop(0, NJ)
        def _(j):
            fetch(side, j).wait()
            term = lax.dot_general(
                held[side * NJ + j],
                act_ref[...],
                (((0,), (0,)), ((), ())),
                preferred_element_type=F32,
            )
            scale = (jnp.max(jnp.abs(term), axis=1, keepdims=True) + 1e-06) / 127.0
            codes = jnp.clip(term * (1.0 / scale), -127.0, 127.0).astype(BF16)
            made[...] = (codes.astype(F32) * scale).astype(BF16)
            for s in range(NX):
                base = lax.rem(x + s, NX) * (NC * OWN)
                mine = pl.multiple_of(base + c * OWN, OWN)
                other = pl.multiple_of(base + (1 - c) * OWN, OWN)
                keeps[side][s, j] = made[pl.ds(mine, OWN), :]
                sends[side][s, j] = made[pl.ds(other, OWN), :]

    for copy in act_copies:
        copy.wait()


def make_terms(pre_act, grad_hidden, inputs):
    out = jax.ShapeDtypeStruct((NX, NJ, OWN, HID), BF16)
    vmem = pl.BlockSpec(memory_space=pltpu.VMEM)
    hbm = pl.BlockSpec(memory_space=pltpu.HBM)
    return pl.pallas_call(
        term_kernel,
        in_specs=[hbm, hbm, hbm],
        out_specs=[vmem] * 4 + [hbm, vmem],
        out_shape=[out] * 4
        + [jax.ShapeDtypeStruct((NT, TOK, HID), BF16), jax.ShapeDtypeStruct((16, 128), BF16)],
        scratch_shapes=[
            pltpu.VMEM((TOK, HID), BF16),
            pltpu.VMEM((TOK, HID), BF16),
            pltpu.VMEM((TOK, HID), BF16),
            pltpu.VMEM((NZ, TOK, ZROWS), BF16),
            pltpu.VMEM((ZROWS, HID), BF16),
            pltpu.SemaphoreType.DMA((NZ + 2 + NT,)),
        ],
        compiler_params=pltpu.CompilerParams(vmem_limit_bytes=56 * 2**20),
        cost_estimate=pl.CostEstimate(
            flops=2 * TOK * D * HID, bytes_accessed=2 * D * (TOK + HID), transcendentals=0
        ),
        name="terms",
    )(pre_act, grad_hidden, inputs)


GI_ROWS = 512
GI_COLS = D // NT


def input_kernel(act_ref, *refs):
    mine_refs, other_refs, out_ref = refs[:NX], refs[NX : 2 * NX], refs[2 * NX]
    x, c, _ = position()
    for w_refs, core in ((mine_refs, c), (other_refs, 1 - c)):
        total = jnp.zeros((GI_ROWS, HALF), F32)
        for s in range(NX):
            total += lax.dot_general(
                act_ref[lax.rem(x + NX - s, NX)],
                w_refs[s][...],
                (((1,), (1,)), ((), ())),
                preferred_element_type=F32,
            )
        out_ref[:, pl.ds(pl.multiple_of(core * HALF, HALF), HALF)] = total.astype(BF16)


def make_grad_input(act_all, mine, other):
    whole = pl.BlockSpec((HALF, HID), lambda i: (0, 0))
    return pl.pallas_call(
        input_kernel,
        grid=(TOK // GI_ROWS,),
        in_specs=[pl.BlockSpec((NT, GI_ROWS, HID), lambda i: (0, i, 0))] + [whole] * (2 * NX),
        out_specs=pl.BlockSpec((GI_ROWS, GI_COLS), lambda i: (i, 0)),
        out_shape=jax.ShapeDtypeStruct((TOK, GI_COLS), BF16),
        compiler_params=pltpu.CompilerParams(vmem_limit_bytes=40 * 2**20),
        cost_estimate=pl.CostEstimate(
            flops=TOK * GI_COLS, bytes_accessed=TOK * GI_COLS, transcendentals=0
        ),
        name="grad_input",
    )(act_all, *mine, *other)


def collect_kernel(*refs):
    pieces, out_ref = refs[:NJ], refs[NJ]
    _, _, z = position()
    for j in range(NJ):
        for side in range(2):
            out_ref[z_of(z, side, NJ - j)] = pieces[j][side]


def collect(pieces):
    return pl.pallas_call(
        collect_kernel,
        out_shape=jax.ShapeDtypeStruct((NZ, OWN, HID), BF16),
        compiler_params=pltpu.CompilerParams(vmem_limit_bytes=4 * 2**20),
        name="collect",
    )(*pieces)


def place_kernel(*refs):
    pieces, out_ref, sems = refs[: 2 * NX], refs[2 * NX], refs[2 * NX + 1]
    x, c, _ = position()
    copies = []
    for s in range(NX):
        from_x = lax.rem(x + NX - s, NX)
        for side, core in ((0, c), (1, 1 - c)):
            copy = pltpu.make_async_copy(
                pieces[2 * s + side], out_ref.at[:, from_x, core], sems.at[2 * s + side]
            )
            copy.start()
            copies.append(copy)
    for copy in copies:
        copy.wait()


def make_weights(pieces):
    out = pl.pallas_call(
        place_kernel,
        in_specs=[pl.BlockSpec(memory_space=pltpu.VMEM)] * (2 * NX),
        out_specs=pl.BlockSpec(memory_space=pl.ANY),
        out_shape=jax.ShapeDtypeStruct((NZ, NX, NC, OWN, HID), BF16),
        scratch_shapes=[pltpu.SemaphoreType.DMA((2 * NX,))],
        compiler_params=pltpu.CompilerParams(vmem_limit_bytes=40 * 2**20),
        name="place",
    )(*pieces)
    return out.reshape(D, HID)


def tie(*arrays):
    return lax.optimization_barrier(arrays)


def spread_kernel(in_ref, after_ref, out_ref):
    for i in range(out_ref.shape[0]):
        out_ref[i] = in_ref[...]


def spread(block, count, after):
    return pl.pallas_call(
        spread_kernel,
        in_specs=[pl.BlockSpec(memory_space=pltpu.VMEM), pl.BlockSpec(memory_space=pl.ANY)],
        out_shape=jax.ShapeDtypeStruct((count,) + block.shape, block.dtype),
        cost_estimate=pl.CostEstimate(flops=10**10, bytes_accessed=0, transcendentals=0),
        compiler_params=pltpu.CompilerParams(vmem_limit_bytes=40 * 2**20),
        name="spread",
    )(block, after)


def sum_kernel(*refs):
    *parts, out_ref = refs
    total = parts[0][...].astype(F32)
    for part in parts[1:]:
        total += part[...].astype(F32)
    out_ref[...] = total.astype(BF16)


def add_parts(*parts):
    return pl.pallas_call(
        sum_kernel,
        out_shape=jax.ShapeDtypeStruct(parts[0].shape, BF16),
        compiler_params=pltpu.CompilerParams(vmem_limit_bytes=8 * 2**20),
        name="add_parts",
    )(*parts)


def swap_all(blocks, axis, groups=None):
    return lax.all_to_all(
        blocks, axis, split_axis=0, concat_axis=0, axis_index_groups=groups, tiled=True
    )


def local(inputs, pre_act, grad_hidden, master, moment_one, moment_two):
    w_own = lax.ppermute(master, ("dp", "tensor"), weight_route())
    *made, act_spread, mark = make_terms(pre_act, grad_hidden, inputs)
    keeps, sends = made[:2], made[2:]
    sends[0], sends[1], w_own = tie(sends[0], sends[1], w_own)
    w_spread = spread(w_own.astype(BF16), NZ, mark)

    sums = [None, None]
    for side in (1, 0):
        recv = lax.ppermute(sends[side], "dp", CORE_SWAP)
        sums[side] = [
            (keeps[side][s].astype(F32) + recv[s].astype(F32)).astype(BF16) for s in range(NX)
        ]
    w_z = swap_all(w_spread, "dp", Z_GROUPS).reshape(HALF, HID)
    parts = [None, None]
    for side in (1, 0):
        parts[side] = [sums[side][0]] + [
            lax.ppermute(sums[side][s], "dp", x_shift(s)) for s in range(1, NX)
        ]
    ahead = add_parts(*parts[1])
    other = lax.ppermute(ahead, "dp", Z_SWAP)
    w_next = spread(w_z, 1, ahead)[0]
    act_spread, w_next = tie(act_spread, w_next)
    act_all = swap_all(act_spread, "tensor")
    total = parts[0][0].astype(F32)
    for part in [*parts[0][1:], other]:
        total += part.astype(F32)
    total = total.astype(BF16)
    w_near = [lax.ppermute(w_next, "dp", x_shift(s)) for s in (1, NX - 1)]
    w_far = lax.ppermute(spread(w_z, 1, total)[0], "dp", x_shift(2))
    others = [lax.ppermute(total[j], "dp", z_shift(2 * j)) for j in range(1, NJ)]
    others[-1], *w_near = tie(others[-1], *w_near)
    grad = total[0].astype(F32)
    for part in others:
        grad += part.astype(F32)

    new_one = 0.9 * moment_one + 0.1 * grad
    new_two = 0.999 * moment_two + 0.001 * grad * grad
    corr_one = 1.0 - 0.9**ADAM_STEP
    corr_two = 1.0 - 0.999**ADAM_STEP
    update = new_one / corr_one / (jnp.sqrt(new_two / corr_two) + 1e-08) + 0.01 * master
    new_master = master - 0.01 * update

    n_own = new_master.astype(BF16)
    n_pair = jnp.stack([n_own, lax.ppermute(n_own, "dp", Z_SWAP)])
    n_z = [n_pair] + [lax.ppermute(n_pair, "dp", z_shift(2 * j)) for j in range(1, NJ)]
    n_z[2], act_all = tie(n_z[2], act_all)
    n_z, w_far = tie(collect(n_z), w_far)
    mine = [n_z] + [lax.ppermute(n_z, "dp", x_shift(s)) for s in range(1, NX)]
    mine[1], w_z, w_far, *w_near = tie(mine[1], w_z, w_far, *w_near)
    w_mine = [w_z, w_near[0], w_far, w_near[1]]
    w_other = [lax.ppermute(piece, "dp", CORE_SWAP) for piece in w_mine]
    grad_input = make_grad_input(act_all, w_mine, w_other)
    pieces = []
    for piece in mine:
        pieces += [piece, lax.ppermute(piece, "dp", CORE_SWAP)]
    grad_input, *pieces = tie(grad_input, *pieces)
    new_weights = make_weights(pieces)
    return (grad_input, new_master, new_one, new_two, new_weights)


def solution(mesh):
    shard = P("dp", "tensor")
    return jax.shard_map(
        local,
        mesh=mesh,
        in_specs=(P("dp", None), shard, shard, shard, shard, shard),
        out_specs=(shard, shard, shard, shard, P(None, "tensor")),
        check_vma=False,
    )
```
